256 devices in a mesh: section: 32 (over x, y, z_lo), dp: 8 (over z_hi, core).
Axes of the slice: x: 4, y: 4, z: 8 (z_hi: 4, z_lo: 2; z = z_hi * 2 + z_lo), core: 2. Of those that a mesh axis runs over, the one named last changes fastest.
Arguments:
- pipe_maps: bfloat16 [32, 8, 8, 32, 384], P('section', 'dp'), may hold values from -6 to 6
- fresh_maps: bfloat16 [3, 8, 8, 32, 384], P(None, 'dp'), may hold values from -6 to 6
- teacher_weight: bfloat16 [64, 3, 3, 384, 384], P('section'), may hold values from -0.109375 to 0.109375
- student_depth: float32 [64, 49, 384], P('section'), may hold values from -0.875 to 0.875
- student_point: bfloat16 [64, 384, 384], P('section'), may hold values from -0.3125 to 0.3125
Outputs:
- final_maps: bfloat16 [32, 8, 8, 32, 384], P('section', 'dp')
- point_grad: float32 [64, 384, 384], P('section', None, 'dp')
- depth_grad: float32 [64, 49, 384], P('section', None, 'dp')
The draws below stay inside these ranges and needn't reach their ends.
All inputs are finite; a program needn't handle non-finite values.
Results may differ from the reference program's by a relative error of at most 0.012.
Values may be sent and summed in bfloat16 or wider, within the bound.
No kernel may reach another device: no remote copies, remote signals or barrier semaphores. Data moves between devices by JAX's collectives and lax.ppermute only.
A program may use at most 128 MiB of HBM per device.

```python
import jax
import jax.numpy as jnp
from jax import lax

CHANNELS = 384
MAP_H = 8
MAP_W = 32
TAPS = 49
TICKS = 4
BATCH = 8
SECTIONS = 32


def block_scale(rng, extent, shards, smallest, largest):
    gain, own = 1.0, jax.random.fold_in(rng, 6)
    for position, blocks in shards:
        steps = jnp.exp(jax.random.uniform(jax.random.fold_in(own, position), (blocks,), jnp.float32, smallest / len(shards), largest / len(shards)))
        gain = gain * jnp.repeat(steps, extent[position] // blocks).reshape([-1 if axis == position else 1 for axis in range(len(extent))])
    return gain


def noise(stream_key, shape, deviation, limit, split=(), kind=jnp.bfloat16):
    result = deviation * jax.random.normal(stream_key, shape, jnp.float32)
    if split:
        result = result * block_scale(stream_key, shape, split, -0.22, 0.18)
    return jnp.clip(result, -limit, limit).astype(kind)


def setup_inputs(seed: int = 0) -> dict:
    streams_of = jax.random.split(jax.random.key(seed), 6)
    return {
        "pipe_maps": noise(streams_of[0], (SECTIONS, BATCH, MAP_H, MAP_W, CHANNELS), 1.0, 6.0, ((0, 32), (1, 8))),
        "fresh_maps": noise(streams_of[1], (TICKS - 1, BATCH, MAP_H, MAP_W, CHANNELS), 1.0, 6.0, ((1, 8),)),
        "teacher_weight": noise(streams_of[2], (2 * SECTIONS, 3, 3, CHANNELS, CHANNELS), (9 * CHANNELS) ** -0.5, 0.109375, ((0, 32),)),
        "student_depth": noise(streams_of[3], (2 * SECTIONS, TAPS, CHANNELS), TAPS ** -0.5, 0.875, ((0, 32),), jnp.float32),
        "student_point": noise(streams_of[4], (2 * SECTIONS, CHANNELS, CHANNELS), CHANNELS ** -0.5, 0.3125, ((0, 32),)),
    }


def teacher_conv(inmap, kernel):
    batch, height, width, chans = inmap.shape
    padded = jnp.pad(inmap, ((0, 0), (1, 1), (1, 1), (0, 0)))
    total = jnp.zeros((batch * height * width, kernel.shape[-1]), jnp.float32)
    for row in range(3):
        for col in range(3):
            window = padded[:, row:row + height, col:col + width, :].reshape(-1, chans)
            total = total + jnp.dot(window, kernel[row, col], preferred_element_type=jnp.float32)
    return total.reshape(batch, height, width, kernel.shape[-1])

def teacher_pass(inmap, kernels):
    hidden = jnp.maximum(teacher_conv(inmap, kernels[0]), 0.0).astype(jnp.bfloat16)
    summed = inmap.astype(jnp.float32) + teacher_conv(hidden, kernels[1])
    return (0.8 * summed).astype(jnp.bfloat16)

def depth_conv(inmap, taps):
    height, width = (inmap.shape[1], inmap.shape[2])
    padded = jnp.pad(inmap, ((0, 0), (3, 3), (3, 3), (0, 0)))
    total = jnp.zeros(inmap.shape, jnp.float32)
    for row in range(7):
        for col in range(7):
            total = total + padded[:, row:row + height, col:col + width, :] * taps[row * 7 + col]
    return total

def point_apply(gelled, weight):
    chans = weight.shape[0]
    flat = jnp.dot(gelled.reshape(-1, chans), weight, preferred_element_type=jnp.float32)
    return flat.reshape(gelled.shape)

def weight_grad(gelled, upstream):
    chans = gelled.shape[-1]
    return lax.dot_general(gelled.reshape(-1, chans), upstream.reshape(-1, chans), (((0,), (0,)), ((), ())), preferred_element_type=jnp.float32)

def block_back(start_map, act_map, upstream, taps, weight):
    up_bf = upstream.astype(jnp.bfloat16)
    gelled = jax.nn.gelu(act_map).astype(jnp.bfloat16)
    point_part = weight_grad(gelled, up_bf)
    dgel = point_apply(up_bf, weight.T)
    dact = jax.vjp(jax.nn.gelu, act_map)[1](dgel)[0]
    back_map, back_taps = jax.vjp(depth_conv, start_map, taps)[1](dact)
    return (point_part, back_taps, upstream + back_map)

def student_grads(inmap, teach, depth, point):
    area = inmap.shape[1] * inmap.shape[2]
    start_zero = inmap.astype(jnp.float32)
    act_zero = depth_conv(start_zero, depth[0])
    start_one = start_zero + point_apply(jax.nn.gelu(act_zero).astype(jnp.bfloat16), point[0])
    act_one = depth_conv(start_one, depth[1])
    final_map = start_one + point_apply(jax.nn.gelu(act_one).astype(jnp.bfloat16), point[1])
    resid = (final_map - teach.astype(jnp.float32)) * (4.0 / area)
    point_one, taps_one, back_one = block_back(start_one, act_one, resid, depth[1], point[1])
    point_zero, taps_zero, back_zero = block_back(start_zero, act_zero, back_one, depth[0], point[0])
    return (jnp.stack([point_zero, point_one]), jnp.stack([taps_zero, taps_one]))

def reference(pipe_maps, fresh_maps, teacher_weight, student_depth, student_point):
    chans = teacher_weight.shape[-1]
    section_count = pipe_maps.shape[0]
    kernels = teacher_weight.reshape(section_count, 2, 3, 3, chans, chans)
    depth = student_depth.reshape(section_count, 2, student_depth.shape[1], chans)
    point = student_point.reshape(section_count, 2, chans, chans)
    current = pipe_maps
    point_total = jnp.zeros((section_count, 2, chans, chans), jnp.float32)
    depth_total = jnp.zeros((section_count, 2, student_depth.shape[1], chans), jnp.float32)

    def per_section(packed):
        inmap, kern, taps, weight = packed
        teach = teacher_pass(inmap, kern)
        point_part, depth_part = student_grads(inmap, teach, taps, weight)
        return (teach, point_part, depth_part)
    teach_all = current
    for tick_index in range(TICKS):
        teach_all, point_part, depth_part = lax.map(per_section, (current, kernels, depth, point))
        point_total = point_total + point_part
        depth_total = depth_total + depth_part
        if tick_index + 1 < TICKS:
            current = jnp.concatenate([fresh_maps[tick_index][None], teach_all[:-1]], axis=0)
    return (teach_all, point_total.reshape(2 * section_count, chans, chans), depth_total.reshape(2 * section_count, student_depth.shape[1], chans))
```

```python
import functools

import jax
import jax.numpy as jnp
import numpy as np
from jax import lax
from jax.experimental import pallas as pl
from jax.experimental.pallas import tpu as pltpu
from jax.sharding import PartitionSpec as P

ROWS, COLS, CHANS = 8, 32, 384
PIX = ROWS * COLS
TAPS = 49
LEN_Y, LEN_X = 11, 36
HALF = LEN_Y * LEN_X // 2
PART = 208
FREQ = 2 * PART
SLOT = 64
WIDE = 2 * CHANS + 2 * SLOT
CHIPS = 4
SHARE = CHANS // (2 * CHIPS)

F32, BF16 = jnp.float32, jnp.bfloat16
GELU_C = float(np.sqrt(2.0 / np.pi))
GELU_A = 0.044715


def transforms():
    wy = 2 * np.pi * np.arange(LEN_Y) / LEN_Y
    wx = 2 * np.pi * (np.arange(LEN_X // 2) + 0.5) / LEN_X
    wy, wx = (a.reshape(-1, 1) for a in np.meshgrid(wy, wx, indexing="ij"))
    y, x = (a.reshape(1, -1) for a in np.meshgrid(np.arange(ROWS), np.arange(COLS), indexing="ij"))
    ty, tx = (a.reshape(1, -1) - 3 for a in np.meshgrid(np.arange(7), np.arange(7), indexing="ij"))

    def stacked(top, bottom):
        gap = np.zeros((PART - HALF, top.shape[1]))
        return np.concatenate([top, gap, bottom, gap])

    pixel, tap = wy * y + wx * x, wy * ty + wx * tx
    forward = stacked(np.cos(pixel), -np.sin(pixel))
    taps = stacked(np.cos(tap), np.sin(tap))
    taps = np.pad(taps, ((0, 0), (0, SLOT - TAPS)))
    return forward, forward.T / HALF, taps


def side_shift(value, shift):
    col = lax.broadcasted_iota(jnp.int32, value.shape, 0) % COLS
    moved = pltpu.roll(value, shift % PIX, 0)
    keep = (col >= shift) if shift > 0 else (col < COLS + shift)
    return jnp.where(keep, moved, 0.0)


def fill_windows(win, value):
    win[COLS : COLS + PIX, 0:CHANS] = side_shift(value, 1).astype(BF16)
    win[COLS : COLS + PIX, CHANS : 2 * CHANS] = value.astype(BF16)
    win[COLS : COLS + PIX, 2 * CHANS :] = side_shift(value, -1).astype(BF16)


def teach_map(x, w, win, ready):
    edge = jnp.zeros((COLS, 3 * CHANS), BF16)
    win[0:COLS, :] = edge
    win[COLS + PIX :, :] = edge

    def conv(first):
        total = None
        for dy in range(3):
            ready(first + dy)
            part = jnp.dot(
                win[dy * COLS : dy * COLS + PIX, :], w[first + dy], preferred_element_type=F32
            )
            total = part if total is None else total + part
        return total

    fill_windows(win, x[...].astype(F32))
    fill_windows(win, jnp.maximum(conv(0), 0.0))
    summed = x[...].astype(F32) + conv(3)
    return (0.8 * summed).astype(BF16)


def first_teacher_kernel(x_ref, w_hbm, out_ref, w_ref, win, sem):
    copies = [pltpu.make_async_copy(w_hbm.at[i], w_ref.at[i], sem.at[i]) for i in range(6)]
    for copy in copies:
        copy.start()
    out_ref[...] = teach_map(x_ref, w_ref, win, lambda i: copies[i].wait())


def next_teacher_kernel(tick, moved_ref, fresh_ref, w_ref, after, out_ref, x_ref, win):
    leading = lax.axis_index("section") == 0

    @pl.when(leading)
    def _():
        x_ref[...] = fresh_ref[tick]

    @pl.when(jnp.logical_not(leading))
    def _():
        x_ref[...] = moved_ref[...]

    out_ref[...] = teach_map(x_ref, w_ref, win, lambda i: None)


VMEM = pl.BlockSpec(memory_space=pltpu.VMEM)
MAP = jax.ShapeDtypeStruct((PIX, CHANS), BF16)
WINDOWS = pltpu.VMEM((PIX + 2 * COLS, 3 * CHANS), BF16)
TEACHER_COST = pl.CostEstimate(
    flops=2 * 18 * PIX * CHANS * CHANS, bytes_accessed=2 * 18 * CHANS * CHANS, transcendentals=0
)


def first_teacher(x, weight):
    return pl.pallas_call(
        first_teacher_kernel,
        out_shape=[MAP, jax.ShapeDtypeStruct(weight.shape, BF16)],
        in_specs=[VMEM, pl.BlockSpec(memory_space=pltpu.HBM)],
        out_specs=[VMEM, VMEM],
        scratch_shapes=[WINDOWS, pltpu.SemaphoreType.DMA((6,))],
        compiler_params=pltpu.CompilerParams(vmem_limit_bytes=20 << 20),
        cost_estimate=TEACHER_COST,
        name="teacher",
    )(x, weight)


def next_teacher(tick, moved, fresh, weight, after):
    return pl.pallas_call(
        functools.partial(next_teacher_kernel, tick),
        out_shape=[MAP, MAP],
        in_specs=[VMEM, VMEM, VMEM, pl.BlockSpec(memory_space=pl.ANY)],
        out_specs=[VMEM, VMEM],
        scratch_shapes=[WINDOWS],
        compiler_params=pltpu.CompilerParams(vmem_limit_bytes=20 << 20),
        cost_estimate=TEACHER_COST,
        name="teacher",
    )(moved, fresh, weight, after)


def gelu_parts(act):
    t = jnp.tanh(GELU_C * (act + GELU_A * act * act * act))
    return t, 0.5 * (1.0 + t)


def gelu_slope(act, t):
    inner = GELU_C * (1.0 + 3.0 * GELU_A * act * act)
    return 0.5 * (1.0 + t) + 0.5 * act * (1.0 - t * t) * inner


CUTS = ((0, 256), (256, 384))


def student_kernel(first, last, *refs):
    refs = list(refs)
    x_ref, teach_ref, f_ref, g_ref, point_ref = refs[:5]
    del refs[:5]
    if first:
        tapf_ref, depth_ref = refs[:2]
        del refs[:2]
    else:
        spec_ref, pacc_in, zacc_in = refs[:3]
        del refs[:3]
        if last:
            tapf_ref = refs.pop(0)
    if last:
        keep_ref, give_ref, final_ref = refs[:3]
        out_ref, sem = refs[-2:]
        del refs[:3], refs[-2:]
        final = pltpu.make_async_copy(teach_ref, final_ref, sem)
        final.start()
    else:
        if first:
            spec_ref = refs.pop(0)
        pacc, zacc = refs[:2]
        del refs[:2]
    freq, dfreq, act, gel, u1, low = refs

    if first:
        for b in range(2):
            spec_ref[b] = jnp.dot(
                tapf_ref[:, 0:TAPS],
                depth_ref[:, b, :],
                preferred_element_type=F32,
                precision=lax.Precision.HIGHEST,
            )

    def halves(ref, lo, cut):
        rows = slice(lo, lo + 16)
        other = slice(PART + lo, PART + lo + 16)
        return ref[rows, cut], ref[other, cut]

    def transform(b, src, dst, cut):
        dst[b, :, cut] = jnp.dot(f_ref[...], src, preferred_element_type=F32)

    def back(cut, product):
        for lo in range(0, PART, 16):
            re, im = product(lo)
            low[lo : lo + 16, cut] = re.astype(BF16)
            low[PART + lo : PART + lo + 16, cut] = im.astype(BF16)
        return jnp.dot(g_ref[...], low[:, cut], preferred_element_type=F32)

    def times(lo, b, cut):
        ar, ai = halves(freq.at[b], lo, cut)
        kr, ki = halves(spec_ref.at[b], lo, cut)
        return ar * kr - ai * ki, ar * ki + ai * kr

    def times_conj(lo, b, cut):
        ar, ai = halves(dfreq.at[b], lo, cut)
        kr, ki = halves(spec_ref.at[b], lo, cut)
        return ar * kr + ai * ki, ai * kr - ar * ki

    def forward(b, src):
        for a, z in CUTS:
            cut = slice(a, z)
            transform(b, src[:, cut].astype(BF16), freq, cut)
            act[b, :, cut] = back(cut, lambda lo: times(lo, b, cut))
            for r in range(0, PIX, 32):
                rows = slice(r, r + 32)
                v = act[b, rows, cut]
                _, cdf = gelu_parts(v)
                gel[b, rows, cut] = (v * cdf).astype(BF16)
        return jnp.dot(gel[b], point_ref[b], preferred_element_type=F32)

    u1[...] = x_ref[...].astype(F32) + forward(0, x_ref)
    grad = (u1[...] + forward(1, u1) - teach_ref[...].astype(F32)) * (4.0 / PIX)
    u1[...] = grad

    for b in (1, 0):
        grad_low = u1[...].astype(BF16)
        part = lax.dot_general(
            grad_low, gel[b], (((0,), (0,)), ((), ())), preferred_element_type=F32
        )
        if not first:
            part = part + pacc_in[b]
        if last:
            out_ref[:, b * CHANS : (b + 1) * CHANS] = part.astype(BF16)
        else:
            pacc[b] = part
        for a, z in CUTS:
            cut = slice(a, z)
            dgel = lax.dot_general(
                grad_low, point_ref[b, cut], (((1,), (1,)), ((), ())), preferred_element_type=F32
            )
            v = act[b, :, cut]
            t, _ = gelu_parts(v)
            transform(b, (dgel * gelu_slope(v, t)).astype(BF16), dfreq, cut)
            if b == 1:
                u1[:, cut] = u1[:, cut] + back(cut, lambda lo: times_conj(lo, b, cut))
            for lo in range(0, PART, 16):
                ir, ii = halves(freq.at[b], lo, cut)
                dr, di = halves(dfreq.at[b], lo, cut)
                re, im = ir * dr + ii * di, ir * di - ii * dr
                if not first:
                    zr, zi = halves(zacc_in.at[b], lo, cut)
                    re, im = re + zr, im + zi
                if last:
                    low[lo : lo + 16, cut] = re.astype(BF16)
                    low[PART + lo : PART + lo + 16, cut] = im.astype(BF16)
                else:
                    zacc[b, lo : lo + 16, cut] = re
                    zacc[b, PART + lo : PART + lo + 16, cut] = im
        if last:
            taps = lax.dot_general(
                low[...], tapf_ref[...], (((0,), (0,)), ((), ())), preferred_element_type=F32
            )
            at = 2 * CHANS + b * SLOT
            out_ref[:, at : at + SLOT] = (taps * (1.0 / HALF)).astype(BF16)

    if last:
        core = lax.axis_index("dp") % 2
        for mine in range(2):

            @pl.when(core == mine)
            def _():
                for chip in range(keep_ref.shape[0]):
                    for target, ref in ((mine, keep_ref), (1 - mine, give_ref)):
                        at = (2 * chip + target) * SHARE
                        ref[chip] = out_ref[at : at + SHARE, :]

        final.wait()


def student(first, last, x, teach, consts, point, carried, extra):
    spec = jax.ShapeDtypeStruct((2, FREQ, CHANS), F32)
    pacc = jax.ShapeDtypeStruct((2, CHANS, CHANS), F32)
    args = [x, teach, *consts, point, *carried, *extra]
    if last:
        outs = [jax.ShapeDtypeStruct((CHIPS, SHARE, WIDE), BF16)] * 2 + [MAP]
    else:
        outs = ([spec] if first else []) + [pacc, spec]
    aliases = {} if first or last else {6: 0, 7: 1}
    return pl.pallas_call(
        functools.partial(student_kernel, first, last),
        out_shape=outs,
        in_specs=[VMEM] * len(args),
        out_specs=[VMEM, VMEM, pl.BlockSpec(memory_space=pl.ANY)] if last else [VMEM] * len(outs),
        input_output_aliases=aliases,
        scratch_shapes=[
            pltpu.VMEM((2, FREQ, CHANS), F32),
            pltpu.VMEM((2, FREQ, CHANS), F32),
            pltpu.VMEM((2, PIX, CHANS), F32),
            pltpu.VMEM((2, PIX, CHANS), BF16),
            pltpu.VMEM((PIX, CHANS), F32),
            pltpu.VMEM((FREQ, CHANS), BF16),
        ]
        + ([pltpu.VMEM((CHANS, WIDE), BF16), pltpu.SemaphoreType.DMA] if last else []),
        compiler_params=pltpu.CompilerParams(vmem_limit_bytes=32 << 20),
        cost_estimate=pl.CostEstimate(
            flops=2 * 13 * PIX * CHANS * CHANS,
            bytes_accessed=8 << 20,
            transcendentals=4 * PIX * CHANS,
        ),
        name="student",
    )(*args)


def fold_kernel(keep_ref, got_ref, mine_ref, *give_refs):
    chip = lax.axis_index("dp") // 2

    def block(index):
        return keep_ref[index].astype(F32) + got_ref[index].astype(F32)

    mine_ref[...] = block(chip)
    for ahead, ref in enumerate(give_refs, 1):
        ref[...] = block((chip + ahead) % CHIPS).astype(BF16)


def fold(keep, got):
    block = (SHARE, WIDE)
    return pl.pallas_call(
        fold_kernel,
        out_shape=[jax.ShapeDtypeStruct(block, F32)]
        + [jax.ShapeDtypeStruct(block, BF16)] * (CHIPS - 1),
        in_specs=[VMEM, VMEM],
        out_specs=[VMEM] * CHIPS,
        compiler_params=pltpu.CompilerParams(vmem_limit_bytes=8 << 20),
        name="fold_cores",
    )(keep, got)


def owner_kernel(mine_ref, *refs):
    *got_refs, point_ref, depth_ref = refs
    total = mine_ref[...]
    for ref in got_refs:
        total = total + ref[...].astype(F32)
    for b in range(2):
        point_ref[b] = total[:, b * CHANS : (b + 1) * CHANS]
        at = 2 * CHANS + b * SLOT
        depth_ref[b] = total[:, at : at + TAPS]


def owner(mine, got):
    return pl.pallas_call(
        owner_kernel,
        out_shape=[
            jax.ShapeDtypeStruct((2, SHARE, CHANS), F32),
            jax.ShapeDtypeStruct((2, SHARE, TAPS), F32),
        ],
        in_specs=[VMEM] * CHIPS,
        out_specs=[VMEM, VMEM],
        compiler_params=pltpu.CompilerParams(vmem_limit_bytes=8 << 20),
        name="owner_sum",
    )(mine, *got)


def sum_at_owner(keep, give):
    devices = 2 * CHIPS
    got = lax.ppermute(give, "dp", [(i, i ^ 1) for i in range(devices)])
    mine, *gives = fold(keep, got)
    routes = [[(i, (i + 2 * ahead) % devices) for i in range(devices)] for ahead in (1, 2, 3)]
    got = [lax.ppermute(block, "dp", route) for block, route in zip(gives, routes)]
    point, depth = owner(mine, got)
    return jnp.swapaxes(point, 1, 2), jnp.swapaxes(depth, 1, 2)


def from_behind(block, axis, distance):
    devices = range(lax.axis_size(axis))
    route = [(i - distance, i) for i in devices if i - distance in devices]
    return lax.ppermute(block, axis, route)


def body(pipe_maps, fresh_maps, teacher_weight, student_depth, student_point):
    ticks = fresh_maps.shape[0] + 1
    weight = teacher_weight.reshape(6, 3 * CHANS, CHANS)
    weight = pltpu.with_memory_space_constraint(weight, pltpu.HBM)
    fresh = fresh_maps.reshape(ticks - 1, PIX, CHANS)
    depth = jnp.swapaxes(student_depth, 0, 1)
    forward, inverse, taps = transforms()
    consts = (jnp.asarray(forward, BF16), jnp.asarray(inverse, BF16))
    current = pipe_maps.reshape(PIX, CHANS)
    carried, extra = (), (jnp.asarray(taps, F32), depth)
    for tick in range(ticks):
        first, last = tick == 0, tick == ticks - 1
        if first:
            teach, weight = first_teacher(current, weight)
        else:
            teach, current = next_teacher(tick - 1, moved, fresh, weight, carried[1])
        if not last:
            moved = from_behind(teach, "section", 1)
        if last:
            extra = (jnp.asarray(taps, BF16),)
        result = student(first, last, current, teach, consts, student_point, carried, extra)
        if first:
            spectrum = result[0]
            carried, extra = tuple(result), ()
        else:
            carried = (spectrum, *result)
    keep, give, final = result
    point_total, depth_total = sum_at_owner(keep, give)
    return (final.reshape(1, 1, ROWS, COLS, CHANS), point_total, depth_total)


def solution(mesh):
    placed = (
        P("section", "dp", None, None, None),
        P(None, "dp", None, None, None),
        P("section", None, None, None, None),
        P("section", None, None),
        P("section", None, None),
    )
    return jax.shard_map(
        body,
        mesh=mesh,
        in_specs=placed,
        out_specs=(
            P("section", "dp", None, None, None),
            P("section", None, "dp"),
            P("section", None, "dp"),
        ),
        check_vma=False,
    )
```

```python
import functools

import jax
import jax.numpy as jnp
import numpy as np
from jax import lax
from jax.experimental import pallas as pl
from jax.experimental.pallas import tpu as pltpu
from jax.sharding import PartitionSpec as P

ROWS, COLS, CHANS = 8, 32, 384
PIX = ROWS * COLS
TAPS = 49
LEN_Y, LEN_X = 11, 36
HALF = LEN_Y * LEN_X // 2
PART = 208
FREQ = 2 * PART
SLOT = 64
WIDE = 2 * CHANS + 2 * SLOT
CHIPS = 4
SHARE = CHANS // (2 * CHIPS)

F32, BF16 = jnp.float32, jnp.bfloat16
GELU_C = float(np.sqrt(2.0 / np.pi))
GELU_A = 0.044715


def transforms():
    wy = 2 * np.pi * np.arange(LEN_Y) / LEN_Y
    wx = 2 * np.pi * (np.arange(LEN_X // 2) + 0.5) / LEN_X
    wy, wx = (a.reshape(-1, 1) for a in np.meshgrid(wy, wx, indexing="ij"))
    y, x = (a.reshape(1, -1) for a in np.meshgrid(np.arange(ROWS), np.arange(COLS), indexing="ij"))
    ty, tx = (a.reshape(1, -1) - 3 for a in np.meshgrid(np.arange(7), np.arange(7), indexing="ij"))

    def stacked(top, bottom):
        gap = np.zeros((PART - HALF, top.shape[1]))
        return np.concatenate([top, gap, bottom, gap])

    pixel, tap = wy * y + wx * x, wy * ty + wx * tx
    forward = stacked(np.cos(pixel), -np.sin(pixel))
    taps = stacked(np.cos(tap), np.sin(tap))
    taps = np.pad(taps, ((0, 0), (0, SLOT - TAPS)))
    return forward, forward.T / HALF, taps


def side_shift(value, shift):
    col = lax.broadcasted_iota(jnp.int32, value.shape, 0) % COLS
    moved = pltpu.roll(value, shift % PIX, 0)
    keep = (col >= shift) if shift > 0 else (col < COLS + shift)
    return jnp.where(keep, moved, 0.0)


def fill_windows(win, value):
    win[COLS : COLS + PIX, 0:CHANS] = side_shift(value, 1).astype(BF16)
    win[COLS : COLS + PIX, CHANS : 2 * CHANS] = value.astype(BF16)
    win[COLS : COLS + PIX, 2 * CHANS :] = side_shift(value, -1).astype(BF16)


def teach_map(x, w, win, ready):
    edge = jnp.zeros((COLS, 3 * CHANS), BF16)
    win[0:COLS, :] = edge
    win[COLS + PIX :, :] = edge

    def conv(first):
        total = None
        for dy in range(3):
            ready(first + dy)
            part = jnp.dot(
                win[dy * COLS : dy * COLS + PIX, :], w[first + dy], preferred_element_type=F32
            )
            total = part if total is None else total + part
        return total

    fill_windows(win, x[...].astype(F32))
    fill_windows(win, jnp.maximum(conv(0), 0.0))
    summed = x[...].astype(F32) + conv(3)
    return (0.8 * summed).astype(BF16)


FLIGHT = 2
MORE = 2


def first_teacher_kernel(x_hbm, w_hbm, *refs):
    others = len(refs) // 2 - 3
    out_ref, w_ref, x_ref = refs[others : others + 3]
    win, sem, x_sem = refs[-3:]
    load = pltpu.make_async_copy(x_hbm, x_ref, x_sem)
    load.start()
    pairs = [(w_hbm.at[i], w_ref.at[i]) for i in range(6)]
    pairs += zip(refs[:others], refs[others + 3 : -3])
    copies = [pltpu.make_async_copy(*pair, sem.at[i]) for i, pair in enumerate(pairs)]
    waiting = list(copies)

    def start(count):
        for copy in waiting[:count]:
            copy.start()
        del waiting[:count]

    def ready(i):
        copies[i].wait()
        start(MORE)

    start(FLIGHT)
    load.wait()
    out_ref[...] = teach_map(x_ref, w_ref, win, ready)
    start(len(waiting))
    for copy in copies[6:]:
        copy.wait()


def take_input(tick, refs, fresh_ref, x_ref):
    section = lax.axis_index("section")

    @pl.when(section == 0)
    def _():
        x_ref[...] = fresh_ref[tick]

    for parity, ref in enumerate(refs):

        @pl.when(jnp.logical_and(section != 0, section % len(refs) == len(refs) - 1 - parity))
        def _():
            x_ref[...] = ref[...]


def whole_teacher_kernel(tick, fresh_ref, w_ref, after, *refs):
    *moved, out_ref, x_ref, win = refs
    take_input(tick, moved, fresh_ref, x_ref)
    out_ref[...] = teach_map(x_ref, w_ref, win, lambda i: None)


def odd_teacher_kernel(tick, fresh_ref, w_ref, after, *refs):
    *moved, out_ref, x_ref, win = refs
    take_input(tick, moved, fresh_ref, x_ref)

    @pl.when(lax.axis_index("section") % 2 == 1)
    def _():
        out_ref[...] = teach_map(x_ref, w_ref, win, lambda i: None)


def even_teacher_kernel(x_ref, w_ref, odd_ref, out_ref, win):
    even = lax.axis_index("section") % 2 == 0

    @pl.when(even)
    def _():
        out_ref[...] = teach_map(x_ref, w_ref, win, lambda i: None)

    @pl.when(jnp.logical_not(even))
    def _():
        out_ref[...] = odd_ref[...]


VMEM = pl.BlockSpec(memory_space=pltpu.VMEM)
MAP = jax.ShapeDtypeStruct((PIX, CHANS), BF16)
WINDOWS = pltpu.VMEM((PIX + 2 * COLS, 3 * CHANS), BF16)
TEACHER_COST = pl.CostEstimate(
    flops=2 * 18 * PIX * CHANS * CHANS, bytes_accessed=2 * 18 * CHANS * CHANS, transcendentals=0
)


def first_teacher(x, weight, *others):
    held = [jax.ShapeDtypeStruct(a.shape, a.dtype) for a in (weight, x, *others)]
    args = [pltpu.with_memory_space_constraint(a, pltpu.HBM) for a in (x, weight, *others)]
    return pl.pallas_call(
        first_teacher_kernel,
        out_shape=[MAP, *held],
        in_specs=[pl.BlockSpec(memory_space=pltpu.HBM)] * len(args),
        out_specs=[VMEM] * (1 + len(held)),
        scratch_shapes=[
            WINDOWS,
            pltpu.SemaphoreType.DMA((6 + len(others),)),
            pltpu.SemaphoreType.DMA,
        ],
        compiler_params=pltpu.CompilerParams(vmem_limit_bytes=20 << 20),
        cost_estimate=TEACHER_COST,
        name="teacher",
    )(*args)


def next_teacher(kernel, tick, moved, fresh, weight, after):
    return pl.pallas_call(
        functools.partial(kernel, tick),
        out_shape=[MAP, MAP],
        in_specs=[VMEM, VMEM, pl.BlockSpec(memory_space=pl.ANY)] + [VMEM] * len(moved),
        out_specs=[VMEM, VMEM],
        scratch_shapes=[WINDOWS],
        compiler_params=pltpu.CompilerParams(vmem_limit_bytes=20 << 20),
        cost_estimate=TEACHER_COST,
        name="teacher",
    )(fresh, weight, after, *moved)


def even_teacher(x, weight, odd):
    return pl.pallas_call(
        even_teacher_kernel,
        out_shape=MAP,
        in_specs=[VMEM] * 3,
        out_specs=VMEM,
        scratch_shapes=[WINDOWS],
        compiler_params=pltpu.CompilerParams(vmem_limit_bytes=20 << 20),
        cost_estimate=TEACHER_COST,
        name="teacher_even",
    )(x, weight, odd)


def settled_kernel(x_ref, out_ref):
    out_ref[...] = x_ref[...]


def settled(x):
    return pl.pallas_call(
        settled_kernel,
        out_shape=MAP,
        in_specs=[VMEM],
        out_specs=VMEM,
        compiler_params=pltpu.CompilerParams(vmem_limit_bytes=8 << 20),
        name="settled",
    )(x)


def gelu_and_slope(act):
    square = act * act
    t = jnp.tanh(act * (GELU_C + GELU_C * GELU_A * square))
    half = 0.5 + 0.5 * t
    value = act * half
    return value, half + value * (1.0 - t) * (GELU_C + 3.0 * GELU_C * GELU_A * square)


CUTS = ((0, 384),)


def student_kernel(first, last, *refs):
    refs = list(refs)
    x_ref, teach_ref, f_ref, g_ref, point_ref = refs[:5]
    del refs[:5]
    if first:
        tapf_ref, depth_ref = refs[:2]
        del refs[:2]
    else:
        spec_ref, pacc_in, zacc_in = refs[:3]
        del refs[:3]
        if last:
            tapf_ref = refs.pop(0)
    if last:
        keep_ref, give_ref, final_ref = refs[:3]
        out_ref, sem = refs[-2:]
        del refs[:3], refs[-2:]
        final = pltpu.make_async_copy(teach_ref, final_ref, sem)
        final.start()
    else:
        if first:
            spec_ref = refs.pop(0)
        pacc, zacc = refs[:2]
        del refs[:2]
    freq, dfreq, act, gel, u1, low = refs

    if first:
        for b in range(2):
            spec_ref[b] = jnp.dot(
                tapf_ref[:, 0:TAPS],
                depth_ref[:, b, :],
                preferred_element_type=F32,
                precision=lax.Precision.HIGHEST,
            )

    def halves(ref, lo, cut):
        rows = slice(lo, lo + 16)
        other = slice(PART + lo, PART + lo + 16)
        return ref[rows, cut], ref[other, cut]

    def transform(b, src, dst, cut):
        dst[b, :, cut] = jnp.dot(f_ref[...], src, preferred_element_type=F32)

    def back(cut, product):
        for lo in range(0, PART, 16):
            re, im = product(lo)
            low[lo : lo + 16, cut] = re.astype(BF16)
            low[PART + lo : PART + lo + 16, cut] = im.astype(BF16)
        return jnp.dot(g_ref[...], low[:, cut], preferred_element_type=F32)

    def times(lo, b, cut):
        ar, ai = halves(freq.at[b], lo, cut)
        kr, ki = halves(spec_ref.at[b], lo, cut)
        return ar * kr - ai * ki, ar * ki + ai * kr

    def times_conj(lo, b, cut):
        ar, ai = halves(dfreq.at[b], lo, cut)
        kr, ki = halves(spec_ref.at[b], lo, cut)
        return ar * kr + ai * ki, ai * kr - ar * ki

    def forward(b, src):
        for a, z in CUTS:
            cut = slice(a, z)
            transform(b, src[:, cut].astype(BF16), freq, cut)
        for a, z in CUTS:
            cut = slice(a, z)
            act[b, :, cut] = back(cut, lambda lo: times(lo, b, cut))
        for a, z in CUTS:
            cut = slice(a, z)
            for r in range(0, PIX, 32):
                rows = slice(r, r + 32)
                value, slope = gelu_and_slope(act[b, rows, cut])
                gel[b, rows, cut] = value.astype(BF16)
                act[b, rows, cut] = slope
        return jnp.dot(gel[b], point_ref[b], preferred_element_type=F32)

    u1[...] = x_ref[...].astype(F32) + forward(0, x_ref)
    grad = (u1[...] + forward(1, u1) - teach_ref[...].astype(F32)) * (4.0 / PIX)
    u1[...] = grad

    for b in (1, 0):
        grad_low = u1[...].astype(BF16)
        part = lax.dot_general(
            grad_low, gel[b], (((0,), (0,)), ((), ())), preferred_element_type=F32
        )
        if not first:
            part = part + pacc_in[b]
        if last:
            out_ref[:, b * CHANS : (b + 1) * CHANS] = part.astype(BF16)
        else:
            pacc[b] = part
        for a, z in CUTS:
            cut = slice(a, z)
            dgel = lax.dot_general(
                grad_low, point_ref[b, cut], (((1,), (1,)), ((), ())), preferred_element_type=F32
            )
            transform(b, (dgel * act[b, :, cut]).astype(BF16), dfreq, cut)
            if b == 1:
                u1[:, cut] = u1[:, cut] + back(cut, lambda lo: times_conj(lo, b, cut))
            for lo in range(0, PART, 16):
                ir, ii = halves(freq.at[b], lo, cut)
                dr, di = halves(dfreq.at[b], lo, cut)
                re, im = ir * dr + ii * di, ir * di - ii * dr
                if not first:
                    zr, zi = halves(zacc_in.at[b], lo, cut)
                    re, im = re + zr, im + zi
                if last:
                    low[lo : lo + 16, cut] = re.astype(BF16)
                    low[PART + lo : PART + lo + 16, cut] = im.astype(BF16)
                else:
                    zacc[b, lo : lo + 16, cut] = re
                    zacc[b, PART + lo : PART + lo + 16, cut] = im
        if last:
            taps = lax.dot_general(
                low[...], tapf_ref[...], (((0,), (0,)), ((), ())), preferred_element_type=F32
            )
            at = 2 * CHANS + b * SLOT
            out_ref[:, at : at + SLOT] = (taps * (1.0 / HALF)).astype(BF16)

    if last:
        core = lax.axis_index("dp") % 2
        for mine in range(2):

            @pl.when(core == mine)
            def _():
                for chip in range(keep_ref.shape[0]):
                    for target, ref in ((mine, keep_ref), (1 - mine, give_ref)):
                        at = (2 * chip + target) * SHARE
                        ref[chip] = out_ref[at : at + SHARE, :]

        final.wait()


def student(first, last, x, teach, consts, point, carried, extra):
    spec = jax.ShapeDtypeStruct((2, FREQ, CHANS), F32)
    pacc = jax.ShapeDtypeStruct((2, CHANS, CHANS), F32)
    args = [x, teach, *consts, point, *carried, *extra]
    if last:
        outs = [jax.ShapeDtypeStruct((CHIPS, SHARE, WIDE), BF16)] * 2 + [MAP]
    else:
        outs = ([spec] if first else []) + [pacc, spec]
    aliases = {} if first or last else {6: 0, 7: 1}
    return pl.pallas_call(
        functools.partial(student_kernel, first, last),
        out_shape=outs,
        in_specs=[VMEM] * len(args),
        out_specs=[VMEM, VMEM, pl.BlockSpec(memory_space=pl.ANY)] if last else [VMEM] * len(outs),
        input_output_aliases=aliases,
        scratch_shapes=[
            pltpu.VMEM((2, FREQ, CHANS), F32),
            pltpu.VMEM((2, FREQ, CHANS), F32),
            pltpu.VMEM((2, PIX, CHANS), F32),
            pltpu.VMEM((2, PIX, CHANS), BF16),
            pltpu.VMEM((PIX, CHANS), F32),
            pltpu.VMEM((FREQ, CHANS), BF16),
        ]
        + ([pltpu.VMEM((CHANS, WIDE), BF16), pltpu.SemaphoreType.DMA] if last else []),
        compiler_params=pltpu.CompilerParams(vmem_limit_bytes=32 << 20),
        cost_estimate=pl.CostEstimate(
            flops=2 * 13 * PIX * CHANS * CHANS,
            bytes_accessed=8 << 20,
            transcendentals=4 * PIX * CHANS,
        ),
        name="student",
    )(*args)


def fold_kernel(keep_ref, got_ref, mine_ref, *give_refs):
    chip = lax.axis_index("dp") // 2

    def block(index):
        return keep_ref[index].astype(F32) + got_ref[index].astype(F32)

    mine_ref[...] = block(chip)
    for ahead, ref in enumerate(give_refs, 1):
        ref[...] = block((chip + ahead) % CHIPS).astype(BF16)


def fold(keep, got):
    block = (SHARE, WIDE)
    return pl.pallas_call(
        fold_kernel,
        out_shape=[jax.ShapeDtypeStruct(block, F32)]
        + [jax.ShapeDtypeStruct(block, BF16)] * (CHIPS - 1),
        in_specs=[VMEM, VMEM],
        out_specs=[VMEM] * CHIPS,
        compiler_params=pltpu.CompilerParams(vmem_limit_bytes=8 << 20),
        name="fold_cores",
    )(keep, got)


def owner_kernel(mine_ref, *refs):
    *got_refs, point_ref, depth_ref = refs
    total = mine_ref[...]
    for ref in got_refs:
        total = total + ref[...].astype(F32)
    for b in range(2):
        point_ref[b] = total[:, b * CHANS : (b + 1) * CHANS]
        at = 2 * CHANS + b * SLOT
        depth_ref[b] = total[:, at : at + TAPS]


def owner(mine, got):
    return pl.pallas_call(
        owner_kernel,
        out_shape=[
            jax.ShapeDtypeStruct((2, SHARE, CHANS), F32),
            jax.ShapeDtypeStruct((2, SHARE, TAPS), F32),
        ],
        in_specs=[VMEM] * CHIPS,
        out_specs=[VMEM, VMEM],
        compiler_params=pltpu.CompilerParams(vmem_limit_bytes=8 << 20),
        name="owner_sum",
    )(mine, *got)


def sum_at_owner(keep, give):
    devices = 2 * CHIPS
    got = lax.ppermute(give, "dp", [(i, i ^ 1) for i in range(devices)])
    mine, *gives = fold(keep, got)
    got = []
    for ahead in (2, 3, 1):
        route = [(i, (i + 2 * ahead) % devices) for i in range(devices)]
        got.append(lax.ppermute(gives[ahead - 1], "dp", route))
    point, depth = owner(mine, got)
    return jnp.swapaxes(point, 1, 2), jnp.swapaxes(depth, 1, 2)


def from_behind(block, axis):
    devices = lax.axis_size(axis)
    return lax.ppermute(block, axis, [(i, (i + 1) % devices) for i in range(devices)])


def from_parity(block, axis, parity):
    devices = range(parity, lax.axis_size(axis) - 1, 2)
    return lax.ppermute(block, axis, [(i, i + 1) for i in devices])


def body(pipe_maps, fresh_maps, teacher_weight, student_depth, student_point):
    ticks = fresh_maps.shape[0] + 1
    weight = teacher_weight.reshape(6, 3 * CHANS, CHANS)
    fresh = fresh_maps.reshape(ticks - 1, PIX, CHANS)
    depth = jnp.swapaxes(student_depth, 0, 1)
    forward, inverse, taps = transforms()
    consts = (jnp.asarray(forward, BF16), jnp.asarray(inverse, BF16))
    current = pipe_maps.reshape(PIX, CHANS)
    carried, extra = (), (jnp.asarray(taps, F32), depth)
    for tick in range(ticks):
        first, last = tick == 0, tick == ticks - 1
        if first:
            teach, weight, current, point, *consts = first_teacher(
                current, weight, student_point, *consts
            )
        elif last:
            teach, current = next_teacher(
                whole_teacher_kernel, tick - 1, moved, fresh, weight, carried[1]
            )
        else:
            odd, current = next_teacher(
                odd_teacher_kernel, tick - 1, moved, fresh, weight, carried[1]
            )
            to_even = settled(from_parity(odd, "section", 1))
            teach = even_teacher(current, weight, odd)
            moved = (from_parity(teach, "section", 0), to_even)
        if first:
            moved = (from_behind(teach, "section"),)
        if last:
            extra = (jnp.asarray(taps, BF16),)
        result = student(first, last, current, teach, consts, point, carried, extra)
        if first:
            spectrum = result[0]
            carried, extra = tuple(result), ()
        else:
            carried = (spectrum, *result)
    keep, give, final = result
    point_total, depth_total = sum_at_owner(keep, give)
    return (final.reshape(1, 1, ROWS, COLS, CHANS), point_total, depth_total)


def solution(mesh):
    placed = (
        P("section", "dp", None, None, None),
        P(None, "dp", None, None, None),
        P("section", None, None, None, None),
        P("section", None, None),
        P("section", None, None),
    )
    return jax.shard_map(
        body,
        mesh=mesh,
        in_specs=placed,
        out_specs=(
            P("section", "dp", None, None, None),
            P("section", None, "dp"),
            P("section", None, "dp"),
        ),
        check_vma=False,
    )
```

```python
import functools

import jax
import jax.numpy as jnp
import numpy as np
from jax import lax
from jax.experimental import pallas as pl
from jax.experimental.pallas import tpu as pltpu
from jax.sharding import PartitionSpec as P

ROWS, COLS, CHANS = 8, 32, 384
PIX = ROWS * COLS
TAPS = 49
LEN_Y, LEN_X = 11, 36
HALF = LEN_Y * LEN_X // 2
PART = 208
FREQ = 2 * PART
SLOT = 64
WIDE = 2 * CHANS + 2 * SLOT
CHIPS = 4
SHARE = CHANS // (2 * CHIPS)

F32, BF16 = jnp.float32, jnp.bfloat16
GELU_C = float(np.sqrt(2.0 / np.pi))
GELU_A = 0.044715


def transforms():
    wy = 2 * np.pi * np.arange(LEN_Y) / LEN_Y
    wx = 2 * np.pi * (np.arange(LEN_X // 2) + 0.5) / LEN_X
    wy, wx = (a.reshape(-1, 1) for a in np.meshgrid(wy, wx, indexing="ij"))
    y, x = (a.reshape(1, -1) for a in np.meshgrid(np.arange(ROWS), np.arange(COLS), indexing="ij"))
    ty, tx = (a.reshape(1, -1) - 3 for a in np.meshgrid(np.arange(7), np.arange(7), indexing="ij"))

    def stacked(top, bottom):
        gap = np.zeros((PART - HALF, top.shape[1]))
        return np.concatenate([top, gap, bottom, gap])

    pixel, tap = wy * y + wx * x, wy * ty + wx * tx
    forward = stacked(np.cos(pixel), -np.sin(pixel))
    taps = stacked(np.cos(tap), np.sin(tap))
    taps = np.pad(taps, ((0, 0), (0, SLOT - TAPS)))
    return forward, forward.T / HALF, taps


def side_shift(value, shift):
    col = lax.broadcasted_iota(jnp.int32, value.shape, 0) % COLS
    moved = pltpu.roll(value, shift % PIX, 0)
    keep = (col >= shift) if shift > 0 else (col < COLS + shift)
    return jnp.where(keep, moved, 0.0)


def fill_windows(win, value):
    win[COLS : COLS + PIX, 0:CHANS] = side_shift(value, 1).astype(BF16)
    win[COLS : COLS + PIX, CHANS : 2 * CHANS] = value.astype(BF16)
    win[COLS : COLS + PIX, 2 * CHANS :] = side_shift(value, -1).astype(BF16)


def teach_map(x, w, win, ready):
    edge = jnp.zeros((COLS, 3 * CHANS), BF16)
    win[0:COLS, :] = edge
    win[COLS + PIX :, :] = edge

    def conv(first):
        total = None
        for dy in range(3):
            ready(first + dy)
            part = jnp.dot(
                win[dy * COLS : dy * COLS + PIX, :], w[first + dy], preferred_element_type=F32
            )
            total = part if total is None else total + part
        return total

    fill_windows(win, x[...].astype(F32))
    fill_windows(win, jnp.maximum(conv(0), 0.0))
    summed = x[...].astype(F32) + conv(3)
    return (0.8 * summed).astype(BF16)


FLIGHT = 2
MORE = 2


def first_teacher_kernel(x_hbm, w_hbm, *refs):
    others = len(refs) // 2 - 3
    out_ref, w_ref, x_ref = refs[others : others + 3]
    win, sem, x_sem = refs[-3:]
    load = pltpu.make_async_copy(x_hbm, x_ref, x_sem)
    load.start()
    pairs = [(w_hbm.at[i], w_ref.at[i]) for i in range(6)]
    pairs += zip(refs[:others], refs[others + 3 : -3])
    copies = [pltpu.make_async_copy(*pair, sem.at[i]) for i, pair in enumerate(pairs)]
    waiting = list(copies)

    def start(count):
        for copy in waiting[:count]:
            copy.start()
        del waiting[:count]

    def ready(i):
        copies[i].wait()
        start(MORE)

    start(FLIGHT)
    load.wait()
    out_ref[...] = teach_map(x_ref, w_ref, win, ready)
    start(len(waiting))
    for copy in copies[6:]:
        copy.wait()


def take_input(tick, refs, fresh_ref, x_ref):
    section = lax.axis_index("section")

    @pl.when(section == 0)
    def _():
        x_ref[...] = fresh_ref[tick]

    for parity, ref in enumerate(refs):

        @pl.when(jnp.logical_and(section != 0, section % len(refs) == len(refs) - 1 - parity))
        def _():
            x_ref[...] = ref[...]


def whole_teacher_kernel(tick, fresh_ref, w_ref, after, *refs):
    *moved, out_ref, x_ref, win = refs
    take_input(tick, moved, fresh_ref, x_ref)
    out_ref[...] = teach_map(x_ref, w_ref, win, lambda i: None)


def odd_teacher_kernel(tick, fresh_ref, w_ref, after, *refs):
    *moved, out_ref, x_ref, win = refs
    take_input(tick, moved, fresh_ref, x_ref)

    @pl.when(lax.axis_index("section") % 2 == 1)
    def _():
        out_ref[...] = teach_map(x_ref, w_ref, win, lambda i: None)


def even_teacher_kernel(x_ref, w_ref, odd_ref, out_ref, win):
    even = lax.axis_index("section") % 2 == 0

    @pl.when(even)
    def _():
        out_ref[...] = teach_map(x_ref, w_ref, win, lambda i: None)

    @pl.when(jnp.logical_not(even))
    def _():
        out_ref[...] = odd_ref[...]


VMEM = pl.BlockSpec(memory_space=pltpu.VMEM)
MAP = jax.ShapeDtypeStruct((PIX, CHANS), BF16)
WINDOWS = pltpu.VMEM((PIX + 2 * COLS, 3 * CHANS), BF16)
TEACHER_COST = pl.CostEstimate(
    flops=2 * 18 * PIX * CHANS * CHANS, bytes_accessed=2 * 18 * CHANS * CHANS, transcendentals=0
)


def first_teacher(x, weight, *others):
    held = [jax.ShapeDtypeStruct(a.shape, a.dtype) for a in (weight, x, *others)]
    args = [pltpu.with_memory_space_constraint(a, pltpu.HBM) for a in (x, weight, *others)]
    return pl.pallas_call(
        first_teacher_kernel,
        out_shape=[MAP, *held],
        in_specs=[pl.BlockSpec(memory_space=pltpu.HBM)] * len(args),
        out_specs=[VMEM] * (1 + len(held)),
        scratch_shapes=[
            WINDOWS,
            pltpu.SemaphoreType.DMA((6 + len(others),)),
            pltpu.SemaphoreType.DMA,
        ],
        compiler_params=pltpu.CompilerParams(vmem_limit_bytes=20 << 20),
        cost_estimate=TEACHER_COST,
        name="teacher",
    )(*args)


def next_teacher(kernel, tick, moved, fresh, weight, after):
    return pl.pallas_call(
        functools.partial(kernel, tick),
        out_shape=[MAP, MAP],
        in_specs=[VMEM, VMEM, pl.BlockSpec(memory_space=pl.ANY)] + [VMEM] * len(moved),
        out_specs=[VMEM, VMEM],
        scratch_shapes=[WINDOWS],
        compiler_params=pltpu.CompilerParams(vmem_limit_bytes=20 << 20),
        cost_estimate=TEACHER_COST,
        name="teacher",
    )(fresh, weight, after, *moved)


def even_teacher(x, weight, odd):
    return pl.pallas_call(
        even_teacher_kernel,
        out_shape=MAP,
        in_specs=[VMEM] * 3,
        out_specs=VMEM,
        scratch_shapes=[WINDOWS],
        compiler_params=pltpu.CompilerParams(vmem_limit_bytes=20 << 20),
        cost_estimate=TEACHER_COST,
        name="teacher_even",
    )(x, weight, odd)


def settled_kernel(x_ref, out_ref):
    out_ref[...] = x_ref[...]


def settled(x):
    return pl.pallas_call(
        settled_kernel,
        out_shape=MAP,
        in_specs=[VMEM],
        out_specs=VMEM,
        compiler_params=pltpu.CompilerParams(vmem_limit_bytes=8 << 20),
        name="settled",
    )(x)


def gelu_and_slope(act):
    square = act * act
    t = jnp.tanh(act * (GELU_C + GELU_C * GELU_A * square))
    half = 0.5 + 0.5 * t
    value = act * half
    return value, half + value * (1.0 - t) * (GELU_C + 3.0 * GELU_C * GELU_A * square)


CUTS = ((0, 384),)


def student_kernel(first, last, *refs):
    refs = list(refs)
    x_ref, teach_ref, f_ref, g_ref, point_ref = refs[:5]
    del refs[:5]
    if first:
        tapf_ref, depth_ref = refs[:2]
        del refs[:2]
    else:
        spec_ref, pacc_in, zacc_in = refs[:3]
        del refs[:3]
        if last:
            tapf_ref = refs.pop(0)
    if last:
        keep_ref, give_ref, final_ref = refs[:3]
        out_ref, sem = refs[-2:]
        del refs[:3], refs[-2:]
        final = pltpu.make_async_copy(teach_ref, final_ref, sem)
        final.start()
    else:
        if first:
            spec_ref = refs.pop(0)
        pacc, zacc = refs[:2]
        del refs[:2]
    freq, dfreq, act, gel, u1, low = refs

    if first:
        for b in range(2):
            spec_ref[b] = jnp.dot(
                tapf_ref[:, 0:TAPS],
                depth_ref[:, b, :],
                preferred_element_type=F32,
                precision=lax.Precision.HIGHEST,
            )

    def halves(ref, lo, cut):
        rows = slice(lo, lo + 16)
        other = slice(PART + lo, PART + lo + 16)
        return ref[rows, cut], ref[other, cut]

    def transform(b, src, dst, cut):
        dst[b, :, cut] = jnp.dot(f_ref[...], src, preferred_element_type=F32)

    def back(cut, product):
        for lo in range(0, PART, 16):
            re, im = product(lo)
            low[lo : lo + 16, cut] = re.astype(BF16)
            low[PART + lo : PART + lo + 16, cut] = im.astype(BF16)
        return jnp.dot(g_ref[...], low[:, cut], preferred_element_type=F32)

    def times(lo, b, cut):
        ar, ai = halves(freq.at[b], lo, cut)
        kr, ki = halves(spec_ref.at[b], lo, cut)
        return ar * kr - ai * ki, ar * ki + ai * kr

    def times_conj(lo, b, cut):
        ar, ai = halves(dfreq.at[b], lo, cut)
        kr, ki = halves(spec_ref.at[b], lo, cut)
        return ar * kr + ai * ki, ai * kr - ar * ki

    def forward(b, src):
        for a, z in CUTS:
            cut = slice(a, z)
            transform(b, src[:, cut].astype(BF16), freq, cut)
        for a, z in CUTS:
            cut = slice(a, z)
            act[b, :, cut] = back(cut, lambda lo: times(lo, b, cut))
        for a, z in CUTS:
            cut = slice(a, z)
            for r in range(0, PIX, 32):
                rows = slice(r, r + 32)
                value, slope = gelu_and_slope(act[b, rows, cut])
                gel[b, rows, cut] = value.astype(BF16)
                act[b, rows, cut] = slope
        return jnp.dot(gel[b], point_ref[b], preferred_element_type=F32)

    u1[...] = x_ref[...].astype(F32) + forward(0, x_ref)
    grad = (u1[...] + forward(1, u1) - teach_ref[...].astype(F32)) * (4.0 / PIX)
    u1[...] = grad

    for b in (1, 0):
        grad_low = u1[...].astype(BF16)
        part = lax.dot_general(
            grad_low, gel[b], (((0,), (0,)), ((), ())), preferred_element_type=F32
        )
        if not first:
            part = part + pacc_in[b]
        if last:
            out_ref[:, b * CHANS : (b + 1) * CHANS] = part.astype(BF16)
        else:
            pacc[b] = part
        for a, z in CUTS:
            cut = slice(a, z)
            dgel = lax.dot_general(
                grad_low, point_ref[b, cut], (((1,), (1,)), ((), ())), preferred_element_type=F32
            )
            transform(b, (dgel * act[b, :, cut]).astype(BF16), dfreq, cut)
            if b == 1:
                u1[:, cut] = u1[:, cut] + back(cut, lambda lo: times_conj(lo, b, cut))
            for lo in range(0, PART, 16):
                ir, ii = halves(freq.at[b], lo, cut)
                dr, di = halves(dfreq.at[b], lo, cut)
                re, im = ir * dr + ii * di, ir * di - ii * dr
                if not first:
                    zr, zi = halves(zacc_in.at[b], lo, cut)
                    re, im = re + zr, im + zi
                if last:
                    low[lo : lo + 16, cut] = re.astype(BF16)
                    low[PART + lo : PART + lo + 16, cut] = im.astype(BF16)
                else:
                    zacc[b, lo : lo + 16, cut] = re
                    zacc[b, PART + lo : PART + lo + 16, cut] = im
        if last:
            taps = lax.dot_general(
                low[...], tapf_ref[...], (((0,), (0,)), ((), ())), preferred_element_type=F32
            )
            at = 2 * CHANS + b * SLOT
            out_ref[:, at : at + SLOT] = (taps * (1.0 / HALF)).astype(BF16)

    if last:
        core = lax.axis_index("dp") % 2
        for mine in range(2):

            @pl.when(core == mine)
            def _():
                for chip in range(keep_ref.shape[0]):
                    for target, ref in ((mine, keep_ref), (1 - mine, give_ref)):
                        at = (2 * chip + target) * SHARE
                        ref[chip] = out_ref[at : at + SHARE, :]

        final.wait()


def student(first, last, x, teach, consts, point, carried, extra):
    spec = jax.ShapeDtypeStruct((2, FREQ, CHANS), F32)
    pacc = jax.ShapeDtypeStruct((2, CHANS, CHANS), F32)
    args = [x, teach, *consts, point, *carried, *extra]
    if last:
        outs = [jax.ShapeDtypeStruct((CHIPS, SHARE, WIDE), BF16)] * 2 + [MAP]
    else:
        outs = ([spec] if first else []) + [pacc, spec]
    aliases = {} if first or last else {6: 0, 7: 1}
    return pl.pallas_call(
        functools.partial(student_kernel, first, last),
        out_shape=outs,
        in_specs=[VMEM] * len(args),
        out_specs=[VMEM, VMEM, pl.BlockSpec(memory_space=pl.ANY)] if last else [VMEM] * len(outs),
        input_output_aliases=aliases,
        scratch_shapes=[
            pltpu.VMEM((2, FREQ, CHANS), F32),
            pltpu.VMEM((2, FREQ, CHANS), F32),
            pltpu.VMEM((2, PIX, CHANS), F32),
            pltpu.VMEM((2, PIX, CHANS), BF16),
            pltpu.VMEM((PIX, CHANS), F32),
            pltpu.VMEM((FREQ, CHANS), BF16),
        ]
        + ([pltpu.VMEM((CHANS, WIDE), BF16), pltpu.SemaphoreType.DMA] if last else []),
        compiler_params=pltpu.CompilerParams(vmem_limit_bytes=32 << 20),
        cost_estimate=pl.CostEstimate(
            flops=2 * 13 * PIX * CHANS * CHANS,
            bytes_accessed=8 << 20,
            transcendentals=4 * PIX * CHANS,
        ),
        name="student",
    )(*args)


def fold_kernel(keep_ref, got_ref, mine_ref, *give_refs):
    chip = lax.axis_index("dp") // 2

    def block(index):
        return keep_ref[index].astype(F32) + got_ref[index].astype(F32)

    mine_ref[...] = block(chip)
    for ahead, ref in enumerate(give_refs, 1):
        ref[...] = block(chip ^ ahead).astype(BF16)


def fold(keep, got):
    block = (SHARE, WIDE)
    return pl.pallas_call(
        fold_kernel,
        out_shape=[jax.ShapeDtypeStruct(block, F32)]
        + [jax.ShapeDtypeStruct(block, BF16)] * (CHIPS - 1),
        in_specs=[VMEM, VMEM],
        out_specs=[VMEM] * CHIPS,
        compiler_params=pltpu.CompilerParams(vmem_limit_bytes=8 << 20),
        name="fold_cores",
    )(keep, got)


def owner_kernel(mine_ref, *refs):
    *got_refs, point_ref, depth_ref = refs
    total = mine_ref[...]
    for ref in got_refs:
        total = total + ref[...].astype(F32)
    for b in range(2):
        point_ref[b] = total[:, b * CHANS : (b + 1) * CHANS]
        at = 2 * CHANS + b * SLOT
        depth_ref[b] = total[:, at : at + TAPS]


def owner(mine, got):
    return pl.pallas_call(
        owner_kernel,
        out_shape=[
            jax.ShapeDtypeStruct((2, SHARE, CHANS), F32),
            jax.ShapeDtypeStruct((2, SHARE, TAPS), F32),
        ],
        in_specs=[VMEM] * CHIPS,
        out_specs=[VMEM, VMEM],
        compiler_params=pltpu.CompilerParams(vmem_limit_bytes=8 << 20),
        name="owner_sum",
    )(mine, *got)


def sum_at_owner(keep, give):
    devices = 2 * CHIPS
    got = lax.ppermute(give, "dp", [(i, i ^ 1) for i in range(devices)])
    mine, *gives = fold(keep, got)
    got = []
    for ahead in (1, 2, 3):
        route = [(i, i ^ (2 * ahead)) for i in range(devices)]
        got.append(lax.ppermute(gives[ahead - 1], "dp", route))
    point, depth = owner(mine, got)
    return jnp.swapaxes(point, 1, 2), jnp.swapaxes(depth, 1, 2)


def from_behind(block, axis):
    devices = lax.axis_size(axis)
    return lax.ppermute(block, axis, [(i, (i + 1) % devices) for i in range(devices)])


def from_parity(block, axis, parity):
    devices = range(parity, lax.axis_size(axis) - 1, 2)
    return lax.ppermute(block, axis, [(i, i + 1) for i in devices])


def body(pipe_maps, fresh_maps, teacher_weight, student_depth, student_point):
    ticks = fresh_maps.shape[0] + 1
    weight = teacher_weight.reshape(6, 3 * CHANS, CHANS)
    fresh = fresh_maps.reshape(ticks - 1, PIX, CHANS)
    depth = jnp.swapaxes(student_depth, 0, 1)
    forward, inverse, taps = transforms()
    consts = (jnp.asarray(forward, BF16), jnp.asarray(inverse, BF16))
    current = pipe_maps.reshape(PIX, CHANS)
    carried, extra = (), (jnp.asarray(taps, F32), depth)
    for tick in range(ticks):
        first, last = tick == 0, tick == ticks - 1
        if first:
            teach, weight, current, point, *consts = first_teacher(
                current, weight, student_point, *consts
            )
        elif last:
            teach, current = next_teacher(
                whole_teacher_kernel, tick - 1, moved, fresh, weight, carried[1]
            )
        else:
            odd, current = next_teacher(
                odd_teacher_kernel, tick - 1, moved, fresh, weight, carried[1]
            )
            to_even = settled(from_parity(odd, "section", 1))
            teach = even_teacher(current, weight, odd)
            moved = (from_parity(teach, "section", 0), to_even)
        if first:
            moved = (from_behind(teach, "section"),)
        if last:
            extra = (jnp.asarray(taps, BF16),)
        result = student(first, last, current, teach, consts, point, carried, extra)
        if first:
            spectrum = result[0]
            carried, extra = tuple(result), ()
        else:
            carried = (spectrum, *result)
    keep, give, final = result
    point_total, depth_total = sum_at_owner(keep, give)
    return (final.reshape(1, 1, ROWS, COLS, CHANS), point_total, depth_total)


def solution(mesh):
    placed = (
        P("section", "dp", None, None, None),
        P(None, "dp", None, None, None),
        P("section", None, None, None, None),
        P("section", None, None),
        P("section", None, None),
    )
    return jax.shard_map(
        body,
        mesh=mesh,
        in_specs=placed,
        out_specs=(
            P("section", "dp", None, None, None),
            P("section", None, "dp"),
            P("section", None, "dp"),
        ),
        check_vma=False,
    )
```

```python
import functools

import jax
import jax.numpy as jnp
import numpy as np
from jax import lax
from jax.experimental import pallas as pl
from jax.experimental.pallas import tpu as pltpu
from jax.sharding import PartitionSpec as P

ROWS, COLS, CHANS = 8, 32, 384
PIX = ROWS * COLS
TAPS = 49
LEN_Y, LEN_X = 11, 36
HALF = LEN_Y * LEN_X // 2
PART = 208
FREQ = 2 * PART
SLOT = 64
WIDE = 2 * CHANS + 2 * SLOT
CHIPS = 4
SHARE = CHANS // (2 * CHIPS)

F32, BF16 = jnp.float32, jnp.bfloat16
GELU_C = float(np.sqrt(2.0 / np.pi))
GELU_A = 0.044715


def transforms():
    wy = 2 * np.pi * np.arange(LEN_Y) / LEN_Y
    wx = 2 * np.pi * (np.arange(LEN_X // 2) + 0.5) / LEN_X
    wy, wx = (a.reshape(-1, 1) for a in np.meshgrid(wy, wx, indexing="ij"))
    y, x = (a.reshape(1, -1) for a in np.meshgrid(np.arange(ROWS), np.arange(COLS), indexing="ij"))
    ty, tx = (a.reshape(1, -1) - 3 for a in np.meshgrid(np.arange(7), np.arange(7), indexing="ij"))

    def stacked(top, bottom):
        gap = np.zeros((PART - HALF, top.shape[1]))
        return np.concatenate([top, gap, bottom, gap])

    pixel, tap = wy * y + wx * x, wy * ty + wx * tx
    forward = stacked(np.cos(pixel), -np.sin(pixel))
    taps = stacked(np.cos(tap), np.sin(tap))
    taps = np.pad(taps, ((0, 0), (0, SLOT - TAPS)))
    return forward, forward.T / HALF, taps


def side_shift(value, shift):
    col = lax.broadcasted_iota(jnp.int32, value.shape, 0) % COLS
    moved = pltpu.roll(value, shift % PIX, 0)
    keep = (col >= shift) if shift > 0 else (col < COLS + shift)
    return jnp.where(keep, moved, 0.0)


def fill_windows(win, value):
    win[COLS : COLS + PIX, 0:CHANS] = side_shift(value, 1).astype(BF16)
    win[COLS : COLS + PIX, CHANS : 2 * CHANS] = value.astype(BF16)
    win[COLS : COLS + PIX, 2 * CHANS :] = side_shift(value, -1).astype(BF16)


def teach_map(x, w, win, ready):
    edge = jnp.zeros((COLS, 3 * CHANS), BF16)
    win[0:COLS, :] = edge
    win[COLS + PIX :, :] = edge

    def conv(first):
        total = None
        for dy in range(3):
            ready(first + dy)
            part = jnp.dot(
                win[dy * COLS : dy * COLS + PIX, :], w[first + dy], preferred_element_type=F32
            )
            total = part if total is None else total + part
        return total

    fill_windows(win, x[...].astype(F32))
    fill_windows(win, jnp.maximum(conv(0), 0.0))
    summed = x[...].astype(F32) + conv(3)
    return (0.8 * summed).astype(BF16)


FLIGHT = 3
MORE = 2


def first_teacher_kernel(x_hbm, w_hbm, *refs):
    others = len(refs) // 2 - 3
    out_ref, w_ref, x_ref = refs[others : others + 3]
    win, sem, x_sem = refs[-3:]
    load = pltpu.make_async_copy(x_hbm, x_ref, x_sem)
    load.start()
    pairs = [(w_hbm.at[i], w_ref.at[i]) for i in range(6)]
    pairs += zip(refs[:others], refs[others + 3 : -3])
    copies = [pltpu.make_async_copy(*pair, sem.at[i]) for i, pair in enumerate(pairs)]
    waiting = list(copies)

    def start(count):
        for copy in waiting[:count]:
            copy.start()
        del waiting[:count]

    def ready(i):
        copies[i].wait()
        start(MORE)

    start(FLIGHT)
    load.wait()
    out_ref[...] = teach_map(x_ref, w_ref, win, ready)
    start(len(waiting))
    for copy in copies[6:]:
        copy.wait()


def take_input(tick, refs, fresh_ref, x_ref):
    section = lax.axis_index("section")

    @pl.when(section == 0)
    def _():
        x_ref[...] = fresh_ref[tick]

    for parity, ref in enumerate(refs):

        @pl.when(jnp.logical_and(section != 0, section % len(refs) == len(refs) - 1 - parity))
        def _():
            x_ref[...] = ref[...]


def whole_teacher_kernel(tick, fresh_ref, w_ref, after, *refs):
    *moved, out_ref, x_ref, win = refs
    take_input(tick, moved, fresh_ref, x_ref)
    out_ref[...] = teach_map(x_ref, w_ref, win, lambda i: None)


def odd_teacher_kernel(tick, fresh_ref, w_ref, after, *refs):
    *moved, out_ref, x_ref, win = refs
    take_input(tick, moved, fresh_ref, x_ref)

    @pl.when(lax.axis_index("section") % 2 == 1)
    def _():
        out_ref[...] = teach_map(x_ref, w_ref, win, lambda i: None)


def even_teacher_kernel(x_ref, w_ref, odd_ref, out_ref, win):
    even = lax.axis_index("section") % 2 == 0

    @pl.when(even)
    def _():
        out_ref[...] = teach_map(x_ref, w_ref, win, lambda i: None)

    @pl.when(jnp.logical_not(even))
    def _():
        out_ref[...] = odd_ref[...]


VMEM = pl.BlockSpec(memory_space=pltpu.VMEM)
MAP = jax.ShapeDtypeStruct((PIX, CHANS), BF16)
WINDOWS = pltpu.VMEM((PIX + 2 * COLS, 3 * CHANS), BF16)
TEACHER_COST = pl.CostEstimate(
    flops=2 * 18 * PIX * CHANS * CHANS, bytes_accessed=2 * 18 * CHANS * CHANS, transcendentals=0
)


def first_teacher(x, weight, *others):
    held = [jax.ShapeDtypeStruct(a.shape, a.dtype) for a in (weight, x, *others)]
    args = [pltpu.with_memory_space_constraint(a, pltpu.HBM) for a in (x, weight, *others)]
    return pl.pallas_call(
        first_teacher_kernel,
        out_shape=[MAP, *held],
        in_specs=[pl.BlockSpec(memory_space=pltpu.HBM)] * len(args),
        out_specs=[VMEM] * (1 + len(held)),
        scratch_shapes=[
            WINDOWS,
            pltpu.SemaphoreType.DMA((6 + len(others),)),
            pltpu.SemaphoreType.DMA,
        ],
        compiler_params=pltpu.CompilerParams(vmem_limit_bytes=20 << 20),
        cost_estimate=TEACHER_COST,
        name="teacher",
    )(*args)


def next_teacher(kernel, tick, moved, fresh, weight, after):
    return pl.pallas_call(
        functools.partial(kernel, tick),
        out_shape=[MAP, MAP],
        in_specs=[VMEM, VMEM, pl.BlockSpec(memory_space=pl.ANY)] + [VMEM] * len(moved),
        out_specs=[VMEM, VMEM],
        scratch_shapes=[WINDOWS],
        compiler_params=pltpu.CompilerParams(vmem_limit_bytes=20 << 20),
        cost_estimate=TEACHER_COST,
        name="teacher",
    )(fresh, weight, after, *moved)


def even_teacher(x, weight, odd):
    return pl.pallas_call(
        even_teacher_kernel,
        out_shape=MAP,
        in_specs=[VMEM] * 3,
        out_specs=VMEM,
        scratch_shapes=[WINDOWS],
        compiler_params=pltpu.CompilerParams(vmem_limit_bytes=20 << 20),
        cost_estimate=TEACHER_COST,
        name="teacher_even",
    )(x, weight, odd)


def settled_kernel(x_ref, out_ref):
    out_ref[...] = x_ref[...]


def settled(x):
    return pl.pallas_call(
        settled_kernel,
        out_shape=MAP,
        in_specs=[VMEM],
        out_specs=VMEM,
        compiler_params=pltpu.CompilerParams(vmem_limit_bytes=8 << 20),
        name="settled",
    )(x)


def gelu_and_slope(act):
    square = act * act
    t = jnp.tanh(act * (GELU_C + GELU_C * GELU_A * square))
    half = 0.5 + 0.5 * t
    value = act * half
    return value, half + value * (1.0 - t) * (GELU_C + 3.0 * GELU_C * GELU_A * square)


CUTS = ((0, 384),)


def student_kernel(first, last, *refs):
    refs = list(refs)
    x_ref, teach_ref, f_ref, g_ref, point_ref = refs[:5]
    del refs[:5]
    if first:
        tapf_ref, depth_ref = refs[:2]
        del refs[:2]
    else:
        spec_ref, pacc_in, zacc_in = refs[:3]
        del refs[:3]
        if last:
            tapf_ref = refs.pop(0)
    if last:
        keep_ref, give_ref, final_ref = refs[:3]
        out_ref, sem = refs[-2:]
        del refs[:3], refs[-2:]
        final = pltpu.make_async_copy(teach_ref, final_ref, sem)
        final.start()
    else:
        if first:
            spec_ref = refs.pop(0)
        pacc, zacc = refs[:2]
        del refs[:2]
    freq, dfreq, act, gel, u1, low = refs

    if first:
        for b in range(2):
            spec_ref[b] = jnp.dot(
                tapf_ref[:, 0:TAPS],
                depth_ref[:, b, :],
                preferred_element_type=F32,
                precision=lax.Precision.HIGHEST,
            )

    def halves(ref, lo, cut):
        rows = slice(lo, lo + 16)
        other = slice(PART + lo, PART + lo + 16)
        return ref[rows, cut], ref[other, cut]

    def transform(b, src, dst, cut):
        dst[b, :, cut] = jnp.dot(f_ref[...], src, preferred_element_type=F32)

    def back(cut, product):
        for lo in range(0, PART, 16):
            re, im = product(lo)
            low[lo : lo + 16, cut] = re.astype(BF16)
            low[PART + lo : PART + lo + 16, cut] = im.astype(BF16)
        return jnp.dot(g_ref[...], low[:, cut], preferred_element_type=F32)

    def times(lo, b, cut):
        ar, ai = halves(freq.at[b], lo, cut)
        kr, ki = halves(spec_ref.at[b], lo, cut)
        return ar * kr - ai * ki, ar * ki + ai * kr

    def times_conj(lo, b, cut):
        ar, ai = halves(dfreq.at[b], lo, cut)
        kr, ki = halves(spec_ref.at[b], lo, cut)
        return ar * kr + ai * ki, ai * kr - ar * ki

    def forward(b, src):
        for a, z in CUTS:
            cut = slice(a, z)
            transform(b, src[:, cut].astype(BF16), freq, cut)
        for a, z in CUTS:
            cut = slice(a, z)
            act[b, :, cut] = back(cut, lambda lo: times(lo, b, cut))
        for a, z in CUTS:
            cut = slice(a, z)
            for r in range(0, PIX, 32):
                rows = slice(r, r + 32)
                value, slope = gelu_and_slope(act[b, rows, cut])
                gel[b, rows, cut] = value.astype(BF16)
                act[b, rows, cut] = slope
        return jnp.dot(gel[b], point_ref[b], preferred_element_type=F32)

    u1[...] = x_ref[...].astype(F32) + forward(0, x_ref)
    grad = (u1[...] + forward(1, u1) - teach_ref[...].astype(F32)) * (4.0 / PIX)
    u1[...] = grad

    for b in (1, 0):
        grad_low = u1[...].astype(BF16)
        part = lax.dot_general(
            grad_low, gel[b], (((0,), (0,)), ((), ())), preferred_element_type=F32
        )
        if not first:
            part = part + pacc_in[b]
        if last:
            out_ref[:, b * CHANS : (b + 1) * CHANS] = part.astype(BF16)
        else:
            pacc[b] = part
        for a, z in CUTS:
            cut = slice(a, z)
            dgel = lax.dot_general(
                grad_low, point_ref[b, cut], (((1,), (1,)), ((), ())), preferred_element_type=F32
            )
            transform(b, (dgel * act[b, :, cut]).astype(BF16), dfreq, cut)
            if b == 1:
                u1[:, cut] = u1[:, cut] + back(cut, lambda lo: times_conj(lo, b, cut))
            for lo in range(0, PART, 16):
                ir, ii = halves(freq.at[b], lo, cut)
                dr, di = halves(dfreq.at[b], lo, cut)
                re, im = ir * dr + ii * di, ir * di - ii * dr
                if not first:
                    zr, zi = halves(zacc_in.at[b], lo, cut)
                    re, im = re + zr, im + zi
                if last:
                    low[lo : lo + 16, cut] = re.astype(BF16)
                    low[PART + lo : PART + lo + 16, cut] = im.astype(BF16)
                else:
                    zacc[b, lo : lo + 16, cut] = re
                    zacc[b, PART + lo : PART + lo + 16, cut] = im
        if last:
            taps = lax.dot_general(
                low[...], tapf_ref[...], (((0,), (0,)), ((), ())), preferred_element_type=F32
            )
            at = 2 * CHANS + b * SLOT
            out_ref[:, at : at + SLOT] = (taps * (1.0 / HALF)).astype(BF16)

    if last:
        core = lax.axis_index("dp") % 2
        for mine in range(2):

            @pl.when(core == mine)
            def _():
                for chip in range(keep_ref.shape[0]):
                    for target, ref in ((mine, keep_ref), (1 - mine, give_ref)):
                        at = (2 * chip + target) * SHARE
                        ref[chip] = out_ref[at : at + SHARE, :]

        final.wait()


def student(first, last, x, teach, consts, point, carried, extra):
    spec = jax.ShapeDtypeStruct((2, FREQ, CHANS), F32)
    pacc = jax.ShapeDtypeStruct((2, CHANS, CHANS), F32)
    args = [x, teach, *consts, point, *carried, *extra]
    if last:
        outs = [jax.ShapeDtypeStruct((CHIPS, SHARE, WIDE), BF16)] * 2 + [MAP]
    else:
        outs = ([spec] if first else []) + [pacc, spec]
    aliases = {} if first or last else {6: 0, 7: 1}
    return pl.pallas_call(
        functools.partial(student_kernel, first, last),
        out_shape=outs,
        in_specs=[VMEM] * len(args),
        out_specs=[VMEM, VMEM, pl.BlockSpec(memory_space=pl.ANY)] if last else [VMEM] * len(outs),
        input_output_aliases=aliases,
        scratch_shapes=[
            pltpu.VMEM((2, FREQ, CHANS), F32),
            pltpu.VMEM((2, FREQ, CHANS), F32),
            pltpu.VMEM((2, PIX, CHANS), F32),
            pltpu.VMEM((2, PIX, CHANS), BF16),
            pltpu.VMEM((PIX, CHANS), F32),
            pltpu.VMEM((FREQ, CHANS), BF16),
        ]
        + ([pltpu.VMEM((CHANS, WIDE), BF16), pltpu.SemaphoreType.DMA] if last else []),
        compiler_params=pltpu.CompilerParams(vmem_limit_bytes=32 << 20),
        cost_estimate=pl.CostEstimate(
            flops=2 * 13 * PIX * CHANS * CHANS,
            bytes_accessed=8 << 20,
            transcendentals=4 * PIX * CHANS,
        ),
        name="student",
    )(*args)


def fold_kernel(keep_ref, got_ref, mine_ref, *give_refs):
    chip = lax.axis_index("dp") // 2

    def block(index):
        return keep_ref[index].astype(F32) + got_ref[index].astype(F32)

    mine_ref[...] = block(chip)
    for ahead, ref in enumerate(give_refs, 1):
        ref[...] = block(chip ^ ahead).astype(BF16)


def fold(keep, got):
    block = (SHARE, WIDE)
    return pl.pallas_call(
        fold_kernel,
        out_shape=[jax.ShapeDtypeStruct(block, F32)]
        + [jax.ShapeDtypeStruct(block, BF16)] * (CHIPS - 1),
        in_specs=[VMEM, VMEM],
        out_specs=[VMEM] * CHIPS,
        compiler_params=pltpu.CompilerParams(vmem_limit_bytes=8 << 20),
        name="fold_cores",
    )(keep, got)


def owner_kernel(mine_ref, *refs):
    *got_refs, point_ref, depth_ref = refs
    total = mine_ref[...]
    for ref in got_refs:
        total = total + ref[...].astype(F32)
    for b in range(2):
        point_ref[b] = total[:, b * CHANS : (b + 1) * CHANS]
        at = 2 * CHANS + b * SLOT
        depth_ref[b] = total[:, at : at + TAPS]


def owner(mine, got):
    return pl.pallas_call(
        owner_kernel,
        out_shape=[
            jax.ShapeDtypeStruct((2, SHARE, CHANS), F32),
            jax.ShapeDtypeStruct((2, SHARE, TAPS), F32),
        ],
        in_specs=[VMEM] * CHIPS,
        out_specs=[VMEM, VMEM],
        compiler_params=pltpu.CompilerParams(vmem_limit_bytes=8 << 20),
        name="owner_sum",
    )(mine, *got)


def sum_at_owner(keep, give):
    devices = 2 * CHIPS
    got = lax.ppermute(give, "dp", [(i, i ^ 1) for i in range(devices)])
    mine, *gives = fold(keep, got)
    got = []
    for ahead in (1, 2, 3):
        route = [(i, i ^ (2 * ahead)) for i in range(devices)]
        got.append(lax.ppermute(gives[ahead - 1], "dp", route))
    point, depth = owner(mine, got)
    return jnp.swapaxes(point, 1, 2), jnp.swapaxes(depth, 1, 2)


def from_behind(block, axis):
    devices = lax.axis_size(axis)
    return lax.ppermute(block, axis, [(i, (i + 1) % devices) for i in range(devices)])


def from_parity(block, axis, parity):
    devices = range(parity, lax.axis_size(axis) - 1, 2)
    return lax.ppermute(block, axis, [(i, i + 1) for i in devices])


def body(pipe_maps, fresh_maps, teacher_weight, student_depth, student_point):
    ticks = fresh_maps.shape[0] + 1
    weight = teacher_weight.reshape(6, 3 * CHANS, CHANS)
    fresh = fresh_maps.reshape(ticks - 1, PIX, CHANS)
    depth = jnp.swapaxes(student_depth, 0, 1)
    forward, inverse, taps = transforms()
    consts = (jnp.asarray(forward, BF16), jnp.asarray(inverse, BF16))
    current = pipe_maps.reshape(PIX, CHANS)
    carried, extra = (), (jnp.asarray(taps, F32), depth)
    for tick in range(ticks):
        first, last = tick == 0, tick == ticks - 1
        if first:
            teach, weight, current, point, *consts = first_teacher(
                current, weight, student_point, *consts
            )
        elif last:
            teach, current = next_teacher(
                whole_teacher_kernel, tick - 1, moved, fresh, weight, carried[1]
            )
        else:
            odd, current = next_teacher(
                odd_teacher_kernel, tick - 1, moved, fresh, weight, carried[1]
            )
            to_even = settled(from_parity(odd, "section", 1))
            teach = even_teacher(current, weight, odd)
            moved = (from_parity(teach, "section", 0), to_even)
        if first:
            moved = (from_behind(teach, "section"),)
        if last:
            extra = (jnp.asarray(taps, BF16),)
        result = student(first, last, current, teach, consts, point, carried, extra)
        if first:
            spectrum = result[0]
            carried, extra = tuple(result), ()
        else:
            carried = (spectrum, *result)
    keep, give, final = result
    point_total, depth_total = sum_at_owner(keep, give)
    return (final.reshape(1, 1, ROWS, COLS, CHANS), point_total, depth_total)


def solution(mesh):
    placed = (
        P("section", "dp", None, None, None),
        P(None, "dp", None, None, None),
        P("section", None, None, None, None),
        P("section", None, None),
        P("section", None, None),
    )
    return jax.shard_map(
        body,
        mesh=mesh,
        in_specs=placed,
        out_specs=(
            P("section", "dp", None, None, None),
            P("section", None, "dp"),
            P("section", None, "dp"),
        ),
        check_vma=False,
    )
```
